512 devices in a mesh: expert: 32 (over x_hi, z), ffn: 16 (over y, x_lo, core).
Axes of the slice: x: 4 (x_hi: 2, x_lo: 2; x = x_hi * 2 + x_lo), y: 4, z: 16, core: 2. Of those that a mesh axis runs over, the one named last changes fastest.
Arguments:
- tokens: bfloat16 [4096, 7168], P('expert', 'ffn'), may hold values from -6 to 6
- routes: int32 [4096, 2], P('expert'), may hold values from 0 to 31, all different within a row; in each aligned block of 128 rows (0 to 127, 128 to 255, ...) at most 16 rows name the same one
- gate_w: bfloat16 [32, 7168, 2048], P('expert', None, 'ffn'), may hold values from -0.0625 to 0.0625
- up_w: bfloat16 [32, 7168, 2048], P('expert', None, 'ffn'), may hold values from -0.0625 to 0.0625
- down_w: bfloat16 [32, 128, 2048], P('expert', None, 'ffn'), may hold values from -2.55 to 2.25
- codes: int32 [32, 128, 128], P('expert'), may hold values from 0 to 15
- scales: float32 [32, 128], P('expert'), may hold values from 0.1 to 0.3
- hinv_panel: float32 [32, 128, 2048], P('expert', None, 'ffn'), may hold values from -0.3 to 1.5, as said below
Outputs:
- hessian: float32 [32, 2048, 2048], P('expert', 'ffn')
- panel_errors: float32 [32, 128, 128], P('expert')
- down_out: bfloat16 [32, 128, 2048], P('expert', None, 'ffn')
The draws below stay inside these ranges and needn't reach their ends.
Inputs may be any that keep to these rules, and one draw needn't show every extreme that they name: `routes`: in each aligned block of 128 rows no expert is named by more than 16 rows, a bound that some block reaches; the 2 entries of a row differ; every expert is named by some row. `hinv_panel`: row i is zero in columns below i; its entry in column i lies between 0.5 and 1.5, the others between -0.3 and 0.3.
All inputs are finite; a program needn't handle non-finite values.
Results may differ from the reference program's by a relative error of at most 0.0047.
Values may be sent and summed in bfloat16 or wider, within the bound.
A program may use at most 64 MiB of HBM per device.

```python
import math
import jax
import jax.numpy as jnp
import numpy as np
from jax import lax

D = 7168
FF = 2048
TOK_GRP = 128
DR = 128
TOP = 2
PANEL = 128
EXPERTS = 32
TOKENS = 4096
CAP = 16
N_EXPERT = 32


def grid_common(key):
    code_key = jax.random.fold_in(key, 101)
    step_key = jax.random.fold_in(key, 202)
    grid = jax.random.randint(code_key, (EXPERTS, DR, FF), 0, 16).astype(jnp.int32)
    steps = jnp.exp(jax.random.uniform(step_key, (EXPERTS, DR), jnp.float32, jnp.log(0.1), jnp.log(0.3)))
    return (grid, steps)


def draw_codes(key, part):
    grid, steps = grid_common(key)
    return grid[:, :, :PANEL]


def draw_scales(key, part):
    grid, steps = grid_common(key)
    return steps


def draw_down_w(key, part):
    grid, steps = grid_common(key)
    key = jax.random.fold_in(key, 9)
    noise = jnp.clip(0.2 * jax.random.normal(key, (EXPERTS, DR, FF), jnp.float32), -0.5, 0.5)
    values = steps[:, :, None] * ((grid - 8).astype(jnp.float32) + noise)
    return values.astype(jnp.bfloat16)


def draw_hinv_panel(key, part):
    key = jax.random.fold_in(key, 11)
    first, second = jax.random.split(key)
    shape = (EXPERTS, PANEL, FF)
    off = jnp.clip(0.05 * jax.random.normal(first, shape, jnp.float32), -0.3, 0.3)
    diag = jax.random.uniform(second, (EXPERTS, PANEL, 1), jnp.float32, 0.5, 1.5)
    rowidx = jnp.arange(PANEL)[:, None]
    colidx = jnp.arange(FF)[None, :]
    upper = jnp.where(colidx < rowidx, jnp.zeros_like(off), off)
    return jnp.where(colidx == rowidx, diag, upper)


def block_levels(own_key, dims, cuts, low, top_value):
    level, own = 1.0, jax.random.fold_in(own_key, 6)
    for axis_at, parts in cuts:
        heights = jnp.exp(jax.random.uniform(jax.random.fold_in(own, axis_at), (parts,), jnp.float32, low / len(cuts), top_value / len(cuts)))
        level = level * jnp.repeat(heights, dims[axis_at] // parts).reshape([-1 if axis == axis_at else 1 for axis in range(len(dims))])
    return level


def routed_block(own_key, own, number, rows, amount, top, most, slope):
    order = jax.random.permutation(own_key, amount)
    crowded, usual = shares(amount, rows * top, most, slope, True), shares(amount, rows * top, most, slope, False)
    places = jnp.arange(amount)

    def named(sizes, offset_by):
        used = int((sizes > 0).sum())
        fixed = max(1, used // 4)
        passed = fixed + (places - fixed + offset_by * (used - fixed)) % max(1, amount - fixed)
        return jnp.zeros((amount,), jnp.int32).at[order[jnp.where(places < fixed, places, passed)]].set(jnp.asarray(sizes, jnp.int32))

    sizes = jnp.where(number % 4 == 0, named(crowded, number // 4), named(usual, number - number // 4 - 1))
    mixed = jax.random.permutation(jax.random.fold_in(own, 3), amount)
    source_of, sink = mixed[0:amount // 2 * 2:2], mixed[1:amount // 2 * 2:2]
    slack = jnp.minimum(sizes[source_of] - 1, most - sizes[sink]) // 2
    slack = jnp.where((source_of == order[0]) | (sink == order[0]) | (sizes[sink] == 0), 0, jnp.maximum(slack, 0))
    passed = jax.random.randint(jax.random.fold_in(own, 4), (amount // 2,), 0, 1 << 20) % (slack + 1)
    sizes = sizes.at[source_of].add(-passed).at[sink].add(passed)
    members = jnp.searchsorted(jnp.cumsum(sizes), jnp.arange(rows * top), side="right").astype(jnp.int32)
    table = members.reshape(top, rows).T
    table = table[jax.random.permutation(jax.random.fold_in(own, 1), rows)]
    offset_by = jax.random.randint(jax.random.fold_in(own, 2), (rows, 1), 0, top)
    return jnp.take_along_axis(table, (jnp.arange(top)[None, :] + offset_by) % top, axis=1)


def shares(count, total, bound, skew, full):
    portions = [(1 << 20) // math.isqrt(grade ** skew) + 1 for grade in range(1, count + 1)]
    largest = bound if full else min(bound, max(-(-total // count), total * portions[0] // sum(portions)))
    least = 1 if total - largest >= count - 1 else 0
    counts, spare = [largest] + [least] * (count - 1), total - largest - least * (count - 1)
    while spare > 0:
        candidates = [i for i in range(1, count) if counts[i] < largest] or [i for i in range(1, count) if counts[i] < bound]
        mass, budget = sum([portions[i] for i in candidates]), spare
        for i in candidates:
            extra = min(bound - counts[i], max(1, budget * portions[i] // mass), spare)
            counts[i] = counts[i] + extra
            spare = spare - extra
    return np.array(counts)


def normal_values(rng, dims, scale, limit, pieces=(), kind=jnp.bfloat16):
    gain = block_levels(rng, dims, pieces, -0.22, 0.18) if pieces else 1.0
    drawn = jax.random.normal(rng, dims, jnp.float32) * scale * gain
    return jnp.minimum(jnp.maximum(drawn, -limit), limit).astype(kind)


def setup_inputs(seed: int = 0) -> dict:
    arg_keys = jax.random.split(jax.random.key(seed), 9)
    tokens = normal_values(arg_keys[0], (TOKENS, D), 1.0, 6.0, ((0, 32), (1, 16)))
    routes_keys = jax.random.split(jax.random.fold_in(arg_keys[1], 1), TOKENS // TOK_GRP)
    routes_turns = jax.random.permutation(jax.random.fold_in(arg_keys[1], 3), TOKENS // TOK_GRP)
    routes = jax.vmap(lambda own, number: routed_block(jax.random.fold_in(arg_keys[1], 2), own, number, TOK_GRP, EXPERTS, TOP, CAP, 1))(routes_keys, routes_turns).reshape((TOKENS, TOP))
    gate_w = normal_values(arg_keys[2], (EXPERTS, D, FF), D ** -0.5, 0.0625, ((0, 32), (2, 16)))
    up_w = normal_values(arg_keys[3], (EXPERTS, D, FF), D ** -0.5, 0.0625, ((0, 32), (2, 16)))
    down_w = draw_down_w(jax.random.fold_in(arg_keys[8], 71), 0)
    codes = draw_codes(jax.random.fold_in(arg_keys[8], 71), 0)
    scales = draw_scales(jax.random.fold_in(arg_keys[8], 71), 0)
    hinv_panel = draw_hinv_panel(jax.random.fold_in(arg_keys[8], 71), 0)
    return {"tokens": tokens, "routes": routes, "gate_w": gate_w, "up_w": up_w, "down_w": down_w, "codes": codes, "scales": scales, "hinv_panel": hinv_panel}


def panel_solve(w, q, u):
    target = w - q
    rows_count = target.shape[0]
    width = target.shape[1]
    zero = jnp.zeros((), jnp.int32)

    def column_step(index, err):
        col = jnp.asarray(index).astype(jnp.int32)
        factor_col = lax.dynamic_slice(u, (zero, col), (width, 1))
        pivot = lax.dynamic_slice(u, (col, col), (1, 1))
        rhs = lax.dynamic_slice(target, (zero, col), (rows_count, 1))
        partial_sum = jnp.dot(err, factor_col, precision=lax.Precision.HIGHEST, preferred_element_type=jnp.float32)
        fresh = (rhs - partial_sum) / pivot
        return lax.dynamic_update_slice(err, fresh.astype(err.dtype), (zero, col))

    start = jnp.zeros((rows_count, width), target.dtype)
    return lax.fori_loop(0, width, column_step, start)


def reference(tokens, routes, gate_w, up_w, down_w, codes, scales, hinv_panel):
    count = TOK_GRP * TOP
    blocks = routes.reshape(N_EXPERT, count)
    ids = jnp.arange(EXPERTS).astype(jnp.int32)
    onehot = (blocks[:, :, None] == ids[None, None, :]).astype(jnp.int32)
    ranks = jnp.sum((jnp.cumsum(onehot, axis=1) - onehot) * onehot, axis=2)
    local_tok = (jnp.arange(count) // TOP).astype(jnp.int32)
    base = (jnp.arange(N_EXPERT) * TOK_GRP).astype(jnp.int32)
    slots = jnp.arange(CAP).astype(jnp.int32)

    def expert_hessian(item):
        expert, gate_m, up_m = item
        hit = (blocks == expert)[:, None, :] & (ranks[:, None, :] == slots[None, :, None])
        tok = jnp.sum(jnp.where(hit, local_tok[None, None, :], 0), axis=2).astype(jnp.int32) + base[:, None]
        valid = jnp.any(hit, axis=2).reshape(-1)
        rows = jnp.take(tokens, tok.reshape(-1).astype(jnp.int32), axis=0)
        rows = jnp.where(valid[:, None], rows, jnp.zeros_like(rows))
        gate = jnp.dot(rows, gate_m, preferred_element_type=jnp.float32)
        up = jnp.dot(rows, up_m, preferred_element_type=jnp.float32)
        hidden = (jax.nn.silu(gate) * up).astype(jnp.bfloat16)
        total = jnp.sum(valid.astype(jnp.float32))
        prod = lax.dot_general(hidden, hidden, (((0,), (0,)), ((), ())), preferred_element_type=jnp.float32)
        return prod * (2.0 / total)

    hessian = lax.map(expert_hessian, (ids, gate_w, up_w))

    def expert_panel(item):
        weights, code, scale, factor = item
        quant = scale[:, None] * (code - 8).astype(jnp.float32)
        wide = weights.astype(jnp.float32)
        err = panel_solve(wide[:, :PANEL], quant, factor[:, :PANEL])
        rest = wide - jnp.dot(err, factor, precision=lax.Precision.HIGHEST, preferred_element_type=jnp.float32)
        padded = jnp.concatenate([quant, jnp.zeros((DR, FF - PANEL), jnp.float32)], axis=1)
        colidx = jnp.arange(FF).astype(jnp.int32)
        out = jnp.where(colidx[None, :] < PANEL, padded, rest)
        return err, out.astype(jnp.bfloat16)

    panel_errors, down_out = lax.map(expert_panel, (down_w, codes, scales, hinv_panel))
    return hessian, panel_errors, down_out
```

```python
import jax
import jax.numpy as jnp
from jax import lax
from jax.experimental import pallas as pl
from jax.experimental.pallas import tpu as pltpu
from jax.sharding import PartitionSpec as P

MESH = pl.DeviceIdType.MESH
NZ = 16
NY = 4
CHIPS = 8
CAP = 16
FEAT = 448
WIDE = 896
FLAGGED = 1024
GROUPS = 4
ROWS = 64
CUT = 512
COLS = 128
HID = 256
HCUT = 128
HALF = ROWS // 2
Z_ORDER = (0, 1, 15, 2, 14, 3, 13, 4, 12, 5, 11, 6, 10, 7, 9, 8)

BESIDE_ROOT = (1, 2, 4, 12)

RING = 12
AT_TOK = 0
AT_GATE = 1
AT_UP = 2
AT_PANEL = 3
AT_A2A = 5
AT_ROWS = AT_A2A + NZ
AT_HID = AT_ROWS + RING * GROUPS
AT_SIB = AT_HID + RING * GROUPS
AT_COUNT = AT_SIB + GROUPS
AT_CAST = AT_COUNT + 1
N_RECV = AT_CAST
N_SEND = AT_CAST + 2 * 15


def exact(a, b):
    return jnp.dot(a, b, precision=lax.Precision.HIGHEST, preferred_element_type=jnp.float32)


def kernel(
    routes_at, tokens, gate_w, up_w, down_at, codes_at, scales_at, hinv_at,
    hess, err_out, down_out,
    routes, down_w, codes, scales, hinv,
    tok, packed, rows, weights, hid, u_panel, w_panel, count,
    send, recv, local,
):
    e = lax.axis_index("expert")
    f = lax.axis_index("ffn")
    xh, z = e // NZ, e % NZ
    y, xl, c = f // 4, (f // 2) % 2, f % 2
    chip = f // 2
    xo = 1 - xl
    yp, ym, yo = (y + 1) % NY, (y + 3) % NY, (y + 2) % NY
    sibling = (e, f + 1 - 2 * c)

    def chip_of(yy, xx):
        return yy * 2 + xx

    def peer(yy, xx):
        return (e, yy * 4 + xx * 2 + c)

    def far(z_to):
        return (((xh + c) % 2) * NZ + z_to, f)

    def copy(src, dst, at, device, send_at=None):
        return pltpu.make_async_remote_copy(
            src_ref=src,
            dst_ref=dst,
            send_sem=send.at[at if send_at is None else send_at],
            recv_sem=recv.at[at],
            device_id=device,
            device_id_type=MESH,
        )

    sent = []

    def go(src, dst, at, device):
        copy(src, dst, at, device).start()
        sent.append((src, at))

    def arrived(region, at):
        copy(region, region, at, sibling).wait_recv()

    half = pl.ds(pl.multiple_of(c * FEAT, FEAT), FEAT)
    other_half = pl.ds(pl.multiple_of((1 - c) * FEAT, FEAT), FEAT)
    own_tok = pltpu.make_async_copy(tokens, tok.at[half], local.at[0])
    own_gate = pltpu.make_async_copy(gate_w, weights.at[c, 0], local.at[1])
    own_up = pltpu.make_async_copy(up_w, weights.at[c, 1], local.at[2])
    small = [
        pltpu.make_async_copy(src, dst, local.at[4 + i])
        for i, (src, dst) in enumerate(
            [(routes_at, routes), (hinv_at, hinv), (down_at, down_w), (codes_at, codes), (scales_at, scales)]
        )
    ]
    small[0].start()
    own_tok.start()
    for one in small[1:]:
        one.start()
    own_gate.start()
    own_up.start()

    barrier = pltpu.get_barrier_semaphore()

    def greet(device):
        pl.semaphore_signal(barrier, inc=1, device_id=device, device_id_type=MESH)

    for dz in range(1, NZ):
        greet(far((z + dz) % NZ))

    @pl.when(c == 1)
    def _():
        greet(far(z))

    greet(peer(yp, xl))
    greet(peer(ym, xl))
    greet(peer(y, xo))
    greet(sibling)

    @pl.when(f == 0)
    def _():
        for other in range(1, 16):
            if other not in BESIDE_ROOT:
                greet((e, jnp.int32(other)))

    beside_root = (f == 1) | (f == 2) | (f == 4) | (f == 12)
    apart = (f != 0) & jnp.logical_not(beside_root)

    @pl.when(apart)
    def _():
        greet((e, jnp.int32(0)))

    small[0].wait()
    names = routes[...]
    experts = lax.broadcasted_iota(jnp.int32, (32, 128), 0)
    named = ((names[0:1, :] == experts) | (names[1:2, :] == experts)).astype(jnp.float32)
    earlier = (
        lax.broadcasted_iota(jnp.int32, (128, 128), 0) < lax.broadcasted_iota(jnp.int32, (128, 128), 1)
    ).astype(jnp.bfloat16)
    named_b = named.astype(jnp.bfloat16)
    rank = jnp.dot(named_b, earlier, preferred_element_type=jnp.float32)
    base = ((xh + c) % 2) * NZ
    slot = lax.broadcasted_iota(jnp.int32, (NZ * CAP, 32), 0)
    widen = (lax.broadcasted_iota(jnp.int32, (NZ * CAP, 32), 1) == base + slot // CAP).astype(jnp.bfloat16)
    rank_at = jnp.dot(widen, rank.astype(jnp.bfloat16), preferred_element_type=jnp.float32)
    named_at = jnp.dot(widen, named_b, preferred_element_type=jnp.float32)
    place = (lax.broadcasted_iota(jnp.int32, (NZ * CAP, 128), 0) % CAP).astype(jnp.float32)
    pick = jnp.where(rank_at == place, named_at, 0.0).astype(jnp.bfloat16)

    peers = NZ - 1 + 4

    @pl.when(f == 0)
    def _():
        pl.semaphore_wait(barrier, peers + 15 - len(BESIDE_ROOT))

    @pl.when(beside_root & (c == 0))
    def _():
        pl.semaphore_wait(barrier, peers)

    @pl.when((f == 1) | (apart & (c == 0)))
    def _():
        pl.semaphore_wait(barrier, peers + 1)

    @pl.when(apart & (c == 1))
    def _():
        pl.semaphore_wait(barrier, peers + 2)

    go(tokens, tok.at[half], AT_TOK, sibling)
    go(gate_w, weights.at[c, 0], AT_GATE, sibling)
    go(up_w, weights.at[c, 1], AT_UP, sibling)

    own_tok.wait()
    arrived(tok.at[other_half], AT_TOK)
    packed[:, :, :WIDE] = (
        lax.dot_general(pick, tok[...], (((1,), (1,)), ((), ())), preferred_element_type=jnp.float32)
        .astype(jnp.bfloat16)
        .reshape(NZ, CAP, WIDE)
    )
    packed[:, :, WIDE:] = (
        jnp.dot(pick, jnp.ones((128, 128), jnp.bfloat16), preferred_element_type=jnp.float32)
        .astype(jnp.bfloat16)
        .reshape(NZ, CAP, 128)
    )

    def landing(k):
        return rows.at[k // 4, chip, pl.ds((k % 4) * CAP, CAP), :]

    stay = pltpu.make_async_copy(packed.at[z], landing(0), local.at[3])

    @pl.when(c == 0)
    def _():
        stay.start()

    @pl.when(c == 1)
    def _():
        copy(packed.at[z], landing(0), AT_A2A, far(z)).start()

    for k in range(1, NZ):
        z_to = (z + Z_ORDER[k]) % NZ
        go(packed.at[z_to], landing(k), AT_A2A + k, far(z_to))

    small[1].wait()
    small[2].wait()

    @pl.when(f == 0)
    def _():
        for other in range(1, 16):
            to = (e, jnp.int32(other))
            copy(hinv, u_panel, AT_PANEL, to, AT_CAST + 2 * other - 2).start()
            copy(down_w, w_panel, AT_PANEL + 1, to, AT_CAST + 2 * other - 1).start()
        u_panel[...] = hinv[...]
        w_panel[...] = down_w[...]

    def ring(piece, at, width, cut):
        def part(yy, xx, first=0, count=ROWS, low=True, high=True):
            ref = piece(chip_of(yy, xx))
            start = 0 if low else cut
            stop = width if high else cut
            return ref.at[pl.ds(first, count), pl.ds(start, stop - start)]

        def send_own():
            mine = part(y, xl)
            go(mine, mine, at + 1, peer(yp, xl))
            go(mine, mine, at + 2, peer(ym, xl))
            go(mine, mine, at + 0, peer(y, xo))

        def second():
            arrived(part(y, xo), at + 0)
            low = part(y, xo, high=False)
            go(low, low, at + 5, peer(yp, xl))
            go(low, low, at + 6, peer(ym, xl))
            arrived(part(ym, xl), at + 1)
            on = part(ym, xl, 0, HALF)
            go(on, on, at + 3, peer(yp, xl))
            cross = part(ym, xl, low=False)
            go(cross, cross, at + 9, peer(y, xo))
            arrived(part(yp, xl), at + 2)
            on = part(yp, xl, HALF, HALF)
            go(on, on, at + 4, peer(ym, xl))
            cross = part(yp, xl, low=False)
            go(cross, cross, at + 10, peer(y, xo))

        def third():
            arrived(part(ym, xo, high=False), at + 5)
            on = part(ym, xo, 0, HALF, high=False)
            go(on, on, at + 7, peer(yp, xl))
            arrived(part(yp, xo, high=False), at + 6)
            on = part(yp, xo, HALF, HALF, high=False)
            go(on, on, at + 8, peer(ym, xl))
            arrived(part(yo, xl, 0, HALF), at + 3)
            arrived(part(yo, xl, HALF, HALF), at + 4)
            cross = part(yo, xl, low=False)
            go(cross, cross, at + 11, peer(y, xo))

        def last():
            arrived(part(ym, xo, low=False), at + 9)
            arrived(part(yp, xo, low=False), at + 10)
            arrived(part(yo, xo, 0, HALF, high=False), at + 7)
            arrived(part(yo, xo, HALF, HALF, high=False), at + 8)
            arrived(part(yo, xo, low=False), at + 11)

        return send_own, second, third, last

    def dispatch_arrived(g):
        for k in range(4 * g, 4 * g + 4):
            if k == 0:

                @pl.when(c == 0)
                def _():
                    stay.wait()

                @pl.when(c == 1)
                def _():
                    arrived(landing(0), AT_A2A)
            else:
                arrived(landing(k), AT_A2A + k)

    def hidden_units(g):
        if g == 0:
            own_gate.wait()
            own_up.wait()
            arrived(weights.at[1 - c, 0], AT_GATE)
            arrived(weights.at[1 - c, 1], AT_UP)
        total = jnp.zeros((ROWS, 2 * HID), jnp.float32)
        for s in range(CHIPS):
            span = pl.ds(s * WIDE, WIDE)
            factor = jnp.concatenate(
                [weights[0, 0, span, :], weights[1, 0, span, :], weights[0, 1, span, :], weights[1, 1, span, :]],
                axis=1,
            )
            total += jnp.dot(rows[g, s, :, :WIDE], factor, preferred_element_type=jnp.float32)
        gate, up = total[:, :HID], total[:, HID:]
        hid[c, g, chip] = (gate / (1.0 + jnp.exp(-gate)) * up).astype(jnp.bfloat16)

    def group(g):
        send_own, second, third, last = ring(lambda s: rows.at[g, s], AT_ROWS + RING * g, WIDE, CUT)
        h_own, h_second, h_third, h_last = ring(lambda s: hid.at[c, g, s], AT_HID + RING * g, HID, HCUT)

        def start():
            dispatch_arrived(g)
            send_own()

        def compute():
            last()
            hidden_units(g)
            h_own()

        def pass_on():
            h_last()
            go(hid.at[c, g], hid.at[c, g], AT_SIB + g, sibling)

        def finish():
            arrived(hid.at[1 - c, g], AT_SIB + g)

        return start, second, third, compute, h_second, h_third, pass_on, finish

    def panel():
        @pl.when(f != 0)
        def _():
            arrived(u_panel, AT_PANEL)
            arrived(w_panel, AT_PANEL + 1)

        u = u_panel[...]
        r = lax.broadcasted_iota(jnp.int32, (128, 128), 0)
        q = lax.broadcasted_iota(jnp.int32, (128, 128), 1)
        on_diag = r == q
        inverse = jnp.where(on_diag, 1.0 / jnp.where(on_diag, u, 1.0), 0.0)
        size = 1
        while size < 128:
            block = jnp.where((r // (2 * size) == q // (2 * size)) & (r // size != q // size), u, 0.0)
            inverse = inverse - exact(exact(inverse, block), inverse)
            size *= 2
            yield
        small[3].wait()
        small[4].wait()
        steps = jnp.sum(jnp.where(on_diag, scales[...], 0.0), axis=1, keepdims=True)
        quant = steps * (codes[...] - 8).astype(jnp.float32)
        err = exact(w_panel[...].astype(jnp.float32) - quant, inverse)
        err_out[...] = err
        yield
        rest = down_w[...].astype(jnp.float32) - exact(err, hinv[...])
        down_out[...] = jnp.where(f == 0, quant, rest).astype(jnp.bfloat16)

    stages = [group(g) for g in range(GROUPS)]
    solve = panel()
    for step in range(GROUPS + 7):
        for g in range(GROUPS):
            if 0 <= step - g < 8:
                stages[g][step - g]()
        next(solve, None)

    flags = rows[:, pl.ds(chip, 1), :, WIDE:].astype(jnp.float32).reshape(GROUPS * ROWS, 128)
    count[c] = jnp.broadcast_to(jnp.sum(flags, axis=0, keepdims=True), (8, 128))
    go(count.at[c], count.at[c], AT_COUNT, sibling)

    mine = hid[:, :, pl.ds(chip, 1), :, pl.ds(pl.multiple_of(c * COLS, COLS), COLS)].reshape(512, COLS)
    products = [
        lax.dot_general(
            mine, hid[:, :, s].reshape(512, HID), (((0,), (0,)), ((), ())), preferred_element_type=jnp.float32
        )
        for s in range(CHIPS)
    ]
    arrived(count.at[1 - c], AT_COUNT)
    scale = 2.0 / (count[0, 0:1, :] + count[1, 0:1, :])
    scale = jnp.concatenate([scale, scale], axis=1)
    for s in range(CHIPS):
        hess[:, s * HID : (s + 1) * HID] = products[s] * scale

    for src, at in sent:
        copy(src, src, at, sibling).wait_send()

    @pl.when(c == 1)
    def _():
        copy(packed.at[z], landing(0), AT_A2A, far(z)).wait_send()

    @pl.when(f == 0)
    def _():
        for other in range(1, 16):
            to = (e, jnp.int32(other))
            copy(hinv, u_panel, AT_PANEL, to, AT_CAST + 2 * other - 2).wait_send()
            copy(down_w, w_panel, AT_PANEL + 1, to, AT_CAST + 2 * other - 1).wait_send()


def body(tokens, routes, gate_w, up_w, down_w, codes, scales, hinv_panel):
    vmem = pl.BlockSpec(memory_space=pltpu.VMEM)
    hbm = pl.BlockSpec(memory_space=pltpu.HBM)
    hess, err, down = pl.pallas_call(
        kernel,
        out_shape=(
            jax.ShapeDtypeStruct((COLS, 2048), jnp.float32),
            jax.ShapeDtypeStruct((128, 128), jnp.float32),
            jax.ShapeDtypeStruct((128, 128), jnp.bfloat16),
        ),
        in_specs=[hbm] * 8,
        out_specs=(vmem, vmem, vmem),
        scratch_shapes=[
            pltpu.VMEM((2, 128), jnp.int32),
            pltpu.VMEM((128, 128), jnp.bfloat16),
            pltpu.VMEM((128, 128), jnp.int32),
            pltpu.VMEM((1, 128), jnp.float32),
            pltpu.VMEM((128, 128), jnp.float32),
            pltpu.VMEM((WIDE, 128), jnp.bfloat16),
            pltpu.VMEM((NZ, CAP, FLAGGED), jnp.bfloat16),
            pltpu.VMEM((GROUPS, CHIPS, ROWS, FLAGGED), jnp.bfloat16),
            pltpu.VMEM((2, 2, CHIPS * WIDE, COLS), jnp.bfloat16),
            pltpu.VMEM((2, GROUPS, CHIPS, ROWS, HID), jnp.bfloat16),
            pltpu.VMEM((128, 128), jnp.float32),
            pltpu.VMEM((128, 128), jnp.bfloat16),
            pltpu.VMEM((2, 8, 128), jnp.float32),
            pltpu.SemaphoreType.DMA((N_SEND,)),
            pltpu.SemaphoreType.DMA((N_RECV,)),
            pltpu.SemaphoreType.DMA((9,)),
        ],
        compiler_params=pltpu.CompilerParams(
            collective_id=0, has_side_effects=True, vmem_limit_bytes=62 * 1024 * 1024
        ),
        cost_estimate=pl.CostEstimate(flops=2_200_000_000, bytes_accessed=16_000_000, transcendentals=65536),
        name="calibrate",
    )(routes.T, tokens.T, gate_w[0], up_w[0], down_w[0], codes[0], scales, hinv_panel[0])
    return hess[None], err[None], down[None]


def solution(mesh):
    return jax.shard_map(
        body,
        mesh=mesh,
        in_specs=(
            P("expert", "ffn"),
            P("expert", None),
            P("expert", None, "ffn"),
            P("expert", None, "ffn"),
            P("expert", None, "ffn"),
            P("expert", None, None),
            P("expert", None),
            P("expert", None, "ffn"),
        ),
        out_specs=(P("expert", "ffn", None), P("expert", None, None), P("expert", None, "ffn")),
        check_vma=False,
    )
```

```python
import jax
import jax.numpy as jnp
from jax import lax
from jax.experimental import pallas as pl
from jax.experimental.pallas import tpu as pltpu
from jax.sharding import PartitionSpec as P

MESH = pl.DeviceIdType.MESH
NZ = 16
NY = 4
CHIPS = 8
CAP = 16
FEAT = 448
WIDE = 896
CUT = 512
COLS = 128
HID = 256
HCUT = 128
Z_ORDER = ((0, 1, 15, 14), (2, 3, 13, 12), (4, 5, 11, 10), (6, 8, 7, 9))
GROUPS = len(Z_ORDER)
FIRST = tuple(sum(len(one) for one in Z_ORDER[:g]) for g in range(GROUPS))
ROWS = tuple(len(one) * CAP for one in Z_ORDER)
ROWS_RING = (True, True, True, True)
HID_RING = (True, True, True, False)
LATE = FIRST[-1] * CAP
FROM_ROOT = (2, 4, 6, 8, 10, 12, 14)

SOLVE = -1
RING = 12
AT_TOK = 0
AT_GATE = 1
AT_UP = 2
AT_PANEL = 3
AT_A2A = 5
AT_ROWS = AT_A2A + NZ
AT_HID = AT_ROWS + RING * GROUPS
AT_SIB = AT_HID + RING * GROUPS
AT_COUNT = AT_SIB + GROUPS
AT_TOTAL = AT_COUNT + NZ
AT_CAST = AT_TOTAL + 1
N_RECV = AT_CAST
N_SEND = AT_CAST + 2 * len(FROM_ROOT)
N_LOCAL = 11 + CHIPS


def exact(a, b):
    return jnp.dot(a, b, precision=lax.Precision.HIGHEST, preferred_element_type=jnp.float32)


def kernel(
    routes_at, tokens, gate_w, up_w, down_at, codes_at, scales_at, hinv_at,
    hess_out, err_out, down_out,
    hess, err_v, down_v, routes, down_w, codes, scales, hinv,
    tok, packed, rows, weights, hid, u_panel, w_panel, count, heard, total,
    send, recv, local,
):
    e = lax.axis_index("expert")
    f = lax.axis_index("ffn")
    xh, z = e // NZ, e % NZ
    y, xl, c = f // 4, (f // 2) % 2, f % 2
    chip = f // 2
    xo = 1 - xl
    yp, ym, yo = (y + 1) % NY, (y + 3) % NY, (y + 2) % NY
    sibling = (e, f + 1 - 2 * c)

    def chip_of(yy, xx):
        return yy * 2 + xx

    def peer(yy, xx):
        return (e, yy * 4 + xx * 2 + c)

    def far(z_to):
        return (((xh + c) % 2) * NZ + z_to, f)

    def copy(src, dst, at, device, send_at=None):
        return pltpu.make_async_remote_copy(
            src_ref=src,
            dst_ref=dst,
            send_sem=send.at[at if send_at is None else send_at],
            recv_sem=recv.at[at],
            device_id=device,
            device_id_type=MESH,
        )

    sent = []

    def go(src, dst, at, device):
        copy(src, dst, at, device).start()
        sent.append((src, at))

    def arrived(region, at):
        copy(region, region, at, sibling).wait_recv()

    half = pl.ds(pl.multiple_of(c * FEAT, FEAT), FEAT)
    other_half = pl.ds(pl.multiple_of((1 - c) * FEAT, FEAT), FEAT)
    own_tok = pltpu.make_async_copy(tokens, tok.at[half], local.at[0])
    own_gate = pltpu.make_async_copy(gate_w, weights.at[c, 0], local.at[1])
    own_up = pltpu.make_async_copy(up_w, weights.at[c, 1], local.at[2])
    small = [
        pltpu.make_async_copy(src, dst, local.at[4 + i])
        for i, (src, dst) in enumerate(
            [(routes_at, routes), (hinv_at, hinv), (down_at, down_w), (codes_at, codes), (scales_at, scales)]
        )
    ]
    small[0].start()
    own_tok.start()
    for one in small[1:]:
        one.start()
    own_gate.start()
    own_up.start()

    barrier = pltpu.get_barrier_semaphore()

    def greet(device):
        pl.semaphore_signal(barrier, inc=1, device_id=device, device_id_type=MESH)

    for dz in range(1, NZ):
        greet(far((z + dz) % NZ))

    @pl.when(c == 1)
    def _():
        greet(far(z))

    for yy in (y, yp, ym, yo):
        greet(peer(yy, xo))
    for yy in (yp, ym, yo):
        greet(peer(yy, xl))
    greet(sibling)

    small[0].wait()
    names = routes[...]
    experts = lax.broadcasted_iota(jnp.int32, (32, 128), 0)
    named = ((names[0:1, :] == experts) | (names[1:2, :] == experts)).astype(jnp.float32)
    earlier = (
        lax.broadcasted_iota(jnp.int32, (128, 128), 0) < lax.broadcasted_iota(jnp.int32, (128, 128), 1)
    ).astype(jnp.bfloat16)
    named_b = named.astype(jnp.bfloat16)
    rank = jnp.dot(named_b, earlier, preferred_element_type=jnp.float32)
    base = ((xh + c) % 2) * NZ
    slot = lax.broadcasted_iota(jnp.int32, (NZ * CAP, 32), 0)
    widen = (lax.broadcasted_iota(jnp.int32, (NZ * CAP, 32), 1) == base + slot // CAP).astype(jnp.bfloat16)
    rank_at = jnp.dot(widen, rank.astype(jnp.bfloat16), preferred_element_type=jnp.float32)
    named_at = jnp.dot(widen, named_b, preferred_element_type=jnp.float32)
    place = (lax.broadcasted_iota(jnp.int32, (NZ * CAP, 128), 0) % CAP).astype(jnp.float32)
    pick = jnp.where(rank_at == place, named_at, 0.0).astype(jnp.bfloat16)
    mine_of = (
        lax.broadcasted_iota(jnp.int32, (NZ, 32), 1) == base + lax.broadcasted_iota(jnp.int32, (NZ, 32), 0)
    ).astype(jnp.bfloat16)
    named_mine = jnp.dot(mine_of, named_b, preferred_element_type=jnp.float32)
    count[...] = jnp.dot(
        named_mine.astype(jnp.bfloat16), jnp.ones((128, 128), jnp.bfloat16), preferred_element_type=jnp.float32
    ).reshape(NZ, 1, 128)

    small[1].wait()
    small[2].wait()
    peers = NZ - 1 + CHIPS - 1 + 1

    @pl.when(c == 0)
    def _():
        pl.semaphore_wait(barrier, peers)

    @pl.when(c == 1)
    def _():
        pl.semaphore_wait(barrier, peers + 1)

    go(tokens, tok.at[half], AT_TOK, sibling)

    def cast(other):
        to = (e, jnp.int32(other))
        at = AT_CAST + 2 * FROM_ROOT.index(other)
        return copy(hinv, u_panel, AT_PANEL, to, at), copy(down_w, w_panel, AT_PANEL + 1, to, at + 1)

    @pl.when(f == 0)
    def _():
        for other in FROM_ROOT:
            for one in cast(other):
                one.start()
        u_panel[...] = hinv[...]
        w_panel[...] = down_w[...]

    own_tok.wait()
    arrived(tok.at[other_half], AT_TOK)
    packed[...] = (
        lax.dot_general(pick, tok[...], (((1,), (1,)), ((), ())), preferred_element_type=jnp.float32)
        .astype(jnp.bfloat16)
        .reshape(NZ, CAP, WIDE)
    )
    def landing(block):
        return rows.at[chip, pl.ds(block * CAP, CAP), :]

    def targets():
        for g in range(GROUPS):
            for j, dz in enumerate(Z_ORDER[g]):
                yield FIRST[g] + j, (z + dz) % NZ

    stay = pltpu.make_async_copy(packed.at[z], landing(0), local.at[3])
    cross_over = copy(packed.at[z], landing(0), AT_A2A, far(z))

    @pl.when(c == 0)
    def _():
        stay.start()

    @pl.when(c == 1)
    def _():
        cross_over.start()

    for block, z_to in targets():
        if block:
            go(packed.at[z_to], landing(block), AT_A2A + block, far(z_to))

    go(gate_w, weights.at[c, 0], AT_GATE, sibling)
    go(up_w, weights.at[c, 1], AT_UP, sibling)

    def dispatch_arrived(g):
        for block in range(FIRST[g], FIRST[g] + len(Z_ORDER[g])):
            if block == 0:

                @pl.when(c == 0)
                def _():
                    stay.wait()

                @pl.when(c == 1)
                def _():
                    arrived(landing(0), AT_A2A)
            else:
                arrived(landing(block), AT_A2A + block)

    def panel_to_sibling():
        @pl.when((c == 0) & (f != 0))
        def _():
            arrived(u_panel, AT_PANEL)
            arrived(w_panel, AT_PANEL + 1)

        @pl.when(c == 0)
        def _():
            copy(u_panel, u_panel, AT_PANEL, sibling).start()
            copy(w_panel, w_panel, AT_PANEL + 1, sibling).start()

    def counts_out():
        heard[0] = count[z]
        for block, z_to in targets():
            if block:
                go(count.at[z_to], heard.at[block], AT_COUNT + block, far(z_to))

        @pl.when(c == 1)
        def _():
            copy(count.at[z], heard.at[NZ], AT_COUNT, far(z)).start()

    def ring(piece, at, count_rows, width, cut):
        half_rows = count_rows // 2

        def part(yy, xx, first=0, count=count_rows, low=True, high=True):
            ref = piece(chip_of(yy, xx))
            start = 0 if low else cut
            stop = width if high else cut
            return ref.at[pl.ds(first, count), pl.ds(start, stop - start)]

        def send_own():
            mine = part(y, xl)
            go(mine, mine, at + 1, peer(yp, xl))
            go(mine, mine, at + 2, peer(ym, xl))
            go(mine, mine, at + 0, peer(y, xo))

        def second():
            arrived(part(y, xo), at + 0)
            low = part(y, xo, high=False)
            go(low, low, at + 5, peer(yp, xl))
            go(low, low, at + 6, peer(ym, xl))
            arrived(part(ym, xl), at + 1)
            on = part(ym, xl, 0, half_rows)
            go(on, on, at + 3, peer(yp, xl))
            cross = part(ym, xl, low=False)
            go(cross, cross, at + 9, peer(y, xo))
            arrived(part(yp, xl), at + 2)
            on = part(yp, xl, half_rows, half_rows)
            go(on, on, at + 4, peer(ym, xl))
            cross = part(yp, xl, low=False)
            go(cross, cross, at + 10, peer(y, xo))

        def third():
            arrived(part(ym, xo, high=False), at + 5)
            on = part(ym, xo, 0, half_rows, high=False)
            go(on, on, at + 7, peer(yp, xl))
            arrived(part(yp, xo, high=False), at + 6)
            on = part(yp, xo, half_rows, half_rows, high=False)
            go(on, on, at + 8, peer(ym, xl))
            arrived(part(yo, xl, 0, half_rows), at + 3)
            arrived(part(yo, xl, half_rows, half_rows), at + 4)
            cross = part(yo, xl, low=False)
            go(cross, cross, at + 11, peer(y, xo))

        def last():
            arrived(part(ym, xo, low=False), at + 9)
            arrived(part(yp, xo, low=False), at + 10)
            arrived(part(yo, xo, 0, half_rows, high=False), at + 7)
            arrived(part(yo, xo, half_rows, half_rows, high=False), at + 8)
            arrived(part(yo, xo, low=False), at + 11)

        return send_own, second, third, last

    def straight(piece, at):
        chips = [(dy, dx) for dy in (2, 1, 3, 0) for dx in (1, 0) if (dy, dx) != (0, 0)]

        def send_own():
            mine = piece(chip)
            for dy, dx in chips:
                go(mine, mine, at + dy * 2 + dx - 1, peer((y + dy) % NY, (xl + dx) % 2))

        def last():
            for dy, dx in chips:
                arrived(piece(chip_of((y + NY - dy) % NY, (xl + dx) % 2)), at + dy * 2 + dx - 1)

        def nothing():
            pass

        return send_own, nothing, nothing, last

    def hidden_units(g):
        if g == 0:
            own_gate.wait()
            own_up.wait()
            arrived(weights.at[1 - c, 0], AT_GATE)
            arrived(weights.at[1 - c, 1], AT_UP)
        span_g = pl.ds(FIRST[g] * CAP, ROWS[g])
        sums = jnp.zeros((ROWS[g], 2 * HID), jnp.float32)
        for s in range(CHIPS):
            span = pl.ds(s * WIDE, WIDE)
            factor = jnp.concatenate(
                [weights[0, 0, span, :], weights[1, 0, span, :], weights[0, 1, span, :], weights[1, 1, span, :]],
                axis=1,
            )
            sums += jnp.dot(rows[s, span_g, :], factor, preferred_element_type=jnp.float32)
        gate, up = sums[:, :HID], sums[:, HID:]
        hid[c, chip, span_g, :] = (gate / (1.0 + jnp.exp(-gate)) * up).astype(jnp.bfloat16)

    def group(g):
        span_g = pl.ds(FIRST[g] * CAP, ROWS[g])

        def row_piece(s):
            return rows.at[s, span_g, :]

        def hid_piece(s):
            return hid.at[c, s, span_g, :]

        if ROWS_RING[g]:
            send_own, second, third, last = ring(row_piece, AT_ROWS + RING * g, ROWS[g], WIDE, CUT)
        else:
            send_own, second, third, last = straight(row_piece, AT_ROWS + RING * g)
        if HID_RING[g]:
            h_own, h_second, h_third, h_last = ring(hid_piece, AT_HID + RING * g, ROWS[g], HID, HCUT)
        else:
            h_own, h_second, h_third, h_last = straight(hid_piece, AT_HID + RING * g)

        def start():
            dispatch_arrived(g)
            send_own()

        def compute():
            last()
            hidden_units(g)
            h_own()

        def pass_on():
            h_last()
            mine = hid.at[c, :, span_g, :]
            go(mine, mine, AT_SIB + g, sibling)

        def finish():
            arrived(hid.at[1 - c, :, span_g, :], AT_SIB + g)

        return start, second, third, compute, h_second, h_third, pass_on, finish

    def panel():
        @pl.when(c == 1)
        def _():
            arrived(u_panel, AT_PANEL)
            arrived(w_panel, AT_PANEL + 1)

        u = u_panel[...]
        r = lax.broadcasted_iota(jnp.int32, (128, 128), 0)
        q = lax.broadcasted_iota(jnp.int32, (128, 128), 1)
        on_diag = r == q
        inverse = jnp.where(on_diag, 1.0 / jnp.where(on_diag, u, 1.0), 0.0)
        size = 1
        while size < 128:
            block = jnp.where((r // (2 * size) == q // (2 * size)) & (r // size != q // size), u, 0.0)
            inverse = inverse - exact(exact(inverse, block), inverse)
            size *= 2
            yield
        small[3].wait()
        small[4].wait()
        steps = jnp.sum(jnp.where(on_diag, scales[...], 0.0), axis=1, keepdims=True)
        quant = steps * (codes[...] - 8).astype(jnp.float32)
        err = exact(w_panel[...].astype(jnp.float32) - quant, inverse)
        err_v[...] = err
        yield
        rest = down_w[...].astype(jnp.float32) - exact(err, hinv[...])
        down_v[...] = jnp.where(f == 0, quant, rest).astype(jnp.bfloat16)
        for one in results[:2]:
            one.start()

    columns = [pl.ds(s * HID, HID) for s in range(CHIPS)]
    results = [
        pltpu.make_async_copy(err_v, err_out, local.at[9]),
        pltpu.make_async_copy(down_v, down_out, local.at[10]),
    ] + [
        pltpu.make_async_copy(hess.at[:, columns[s]], hess_out.at[:, columns[s]], local.at[11 + s])
        for s in range(CHIPS)
    ]

    stages = [group(g) for g in range(GROUPS)]
    solve = panel()

    def run(*order):
        for who, what in order:
            if who == SOLVE:
                for _ in range(what):
                    next(solve, None)
            else:
                stages[who][what]()

    def products(start, count):
        def take(cc, at, width_at):
            return hid[cc, at, pl.ds(start, count), width_at]

        own = pl.ds(pl.multiple_of(c * COLS, COLS), COLS)
        mine = jnp.concatenate([take(0, chip, own), take(1, chip, own)], axis=0)
        for s in range(CHIPS):
            both = jnp.concatenate([take(0, s, slice(None)), take(1, s, slice(None))], axis=0)
            yield s, lax.dot_general(mine, both, (((0,), (0,)), ((), ())), preferred_element_type=jnp.float32)

    counts_out()
    run((0, 0))
    panel_to_sibling()
    run(
        (SOLVE, 4), (0, 1), (1, 0), (SOLVE, 2), (0, 2), (1, 1), (2, 0), (SOLVE, 2), (0, 3),
        (1, 2), (2, 1), (3, 0), (SOLVE, 1), (0, 4), (1, 3), (2, 2), (3, 1), (0, 5),
        (1, 4), (2, 3), (3, 2), (0, 6), (1, 5), (2, 4), (3, 3), (1, 6), (2, 5),
        (0, 7), (2, 6), (1, 7), (2, 7),
    )

    for block in range(1, NZ):
        arrived(heard.at[block], AT_COUNT + block)

    @pl.when(c == 1)
    def _():
        arrived(heard.at[NZ], AT_COUNT)

    own_count = jnp.sum(heard[1:NZ, 0], axis=0, keepdims=True) + jnp.where(c == 0, heard[0], heard[NZ])
    total[c] = jnp.broadcast_to(own_count, (8, 128))
    go(total.at[c], total.at[c], AT_TOTAL, sibling)
    for s, product in products(0, LATE):
        hess[:, columns[s]] = product
    run((3, 6))
    arrived(total.at[1 - c], AT_TOTAL)
    scale = 2.0 / (total[0, 0:1, :] + total[1, 0:1, :])
    scale = jnp.concatenate([scale, scale], axis=1)
    run((3, 7))
    for s, product in products(LATE, ROWS[-1]):
        hess[:, columns[s]] = scale * (hess[:, columns[s]] + product)
        results[2 + s].start()

    for src, at in sent:
        copy(src, src, at, sibling).wait_send()

    @pl.when(c == 1)
    def _():
        cross_over.wait_send()
        copy(count.at[z], heard.at[NZ], AT_COUNT, far(z)).wait_send()

    @pl.when(c == 0)
    def _():
        copy(u_panel, u_panel, AT_PANEL, sibling).wait_send()
        copy(w_panel, w_panel, AT_PANEL + 1, sibling).wait_send()

    @pl.when(f == 0)
    def _():
        for other in FROM_ROOT:
            for one in cast(other):
                one.wait_send()

    for one in results:
        one.wait()


def hand_on(hess, err, down, hess_out, err_out, down_out, hess_v, err_v, down_v, in_sems, out_sems):
    part = 32
    trips = [(err, err_v, err_out), (down, down_v, down_out)]
    for i in range(4):
        span = pl.ds(i * part, part)
        trips.append((hess.at[span], hess_v.at[span], hess_out.at[span]))
    loads = [pltpu.make_async_copy(src, here, in_sems.at[i]) for i, (src, here, _) in enumerate(trips)]
    stores = [pltpu.make_async_copy(here, dst, out_sems.at[i]) for i, (_, here, dst) in enumerate(trips)]
    for load in loads:
        load.start()
    for load, store in zip(loads, stores):
        load.wait()
        store.start()
    for store in stores:
        store.wait()


def body(tokens, routes, gate_w, up_w, down_w, codes, scales, hinv_panel):
    hbm = pl.BlockSpec(memory_space=pltpu.HBM)
    outs = (
        jax.ShapeDtypeStruct((COLS, 2048), jnp.float32),
        jax.ShapeDtypeStruct((128, 128), jnp.float32),
        jax.ShapeDtypeStruct((128, 128), jnp.bfloat16),
    )
    done = pl.pallas_call(
        kernel,
        out_shape=outs,
        in_specs=[hbm] * 8,
        out_specs=(hbm,) * 3,
        scratch_shapes=[
            pltpu.VMEM((COLS, 2048), jnp.float32),
            pltpu.VMEM((128, 128), jnp.float32),
            pltpu.VMEM((128, 128), jnp.bfloat16),
            pltpu.VMEM((2, 128), jnp.int32),
            pltpu.VMEM((128, 128), jnp.bfloat16),
            pltpu.VMEM((128, 128), jnp.int32),
            pltpu.VMEM((1, 128), jnp.float32),
            pltpu.VMEM((128, 128), jnp.float32),
            pltpu.VMEM((WIDE, 128), jnp.bfloat16),
            pltpu.VMEM((NZ, CAP, WIDE), jnp.bfloat16),
            pltpu.VMEM((CHIPS, NZ * CAP, WIDE), jnp.bfloat16),
            pltpu.VMEM((2, 2, CHIPS * WIDE, COLS), jnp.bfloat16),
            pltpu.VMEM((2, CHIPS, NZ * CAP, HID), jnp.bfloat16),
            pltpu.VMEM((128, 128), jnp.float32),
            pltpu.VMEM((128, 128), jnp.bfloat16),
            pltpu.VMEM((NZ, 1, 128), jnp.float32),
            pltpu.VMEM((NZ + 1, 1, 128), jnp.float32),
            pltpu.VMEM((2, 8, 128), jnp.float32),
            pltpu.SemaphoreType.DMA((N_SEND,)),
            pltpu.SemaphoreType.DMA((N_RECV,)),
            pltpu.SemaphoreType.DMA((N_LOCAL,)),
        ],
        compiler_params=pltpu.CompilerParams(
            collective_id=0, has_side_effects=True, vmem_limit_bytes=62 * 1024 * 1024
        ),
        cost_estimate=pl.CostEstimate(flops=2_200_000_000, bytes_accessed=16_000_000, transcendentals=65536),
        name="calibrate",
    )(routes.T, tokens.T, gate_w[0], up_w[0], down_w[0], codes[0], scales, hinv_panel[0])
    hess, err, down = pl.pallas_call(
        hand_on,
        out_shape=outs,
        in_specs=[hbm] * 3,
        out_specs=(hbm,) * 3,
        scratch_shapes=[
            pltpu.VMEM((COLS, 2048), jnp.float32),
            pltpu.VMEM((128, 128), jnp.float32),
            pltpu.VMEM((128, 128), jnp.bfloat16),
            pltpu.SemaphoreType.DMA((6,)),
            pltpu.SemaphoreType.DMA((6,)),
        ],
        name="hand_on",
    )(*done)
    return hess[None], err[None], down[None]


def solution(mesh):
    return jax.shard_map(
        body,
        mesh=mesh,
        in_specs=(
            P("expert", "ffn"),
            P("expert", None),
            P("expert", None, "ffn"),
            P("expert", None, "ffn"),
            P("expert", None, "ffn"),
            P("expert", None, None),
            P("expert", None),
            P("expert", None, "ffn"),
        ),
        out_specs=(P("expert", "ffn", None), P("expert", None, None), P("expert", None, "ffn")),
        check_vma=False,
    )
```

```python
import jax
import jax.numpy as jnp
from jax import lax
from jax.experimental import pallas as pl
from jax.experimental.pallas import tpu as pltpu
from jax.sharding import PartitionSpec as P

MESH = pl.DeviceIdType.MESH
NZ = 16
NY = 4
CHIPS = 8
CAP = 16
FEAT = 448
WIDE = 896
CUT = 512
COLS = 128
HID = 256
HCUT = 128
Z_ORDER = ((0, 1, 15, 14), (2, 3, 13, 12), (4, 5, 11, 10), (6, 8, 7, 9))
GROUPS = len(Z_ORDER)
FIRST = tuple(sum(len(one) for one in Z_ORDER[:g]) for g in range(GROUPS))
ROWS = tuple(len(one) * CAP for one in Z_ORDER)
ROWS_RING = (True, True, True, True)
HID_RING = (True, True, True, False)
LATE = FIRST[-1] * CAP
FROM_ROOT = (2, 4, 6, 8, 10, 12, 14)

SOLVE = -1
RING = 12
AT_TOK = 0
AT_GATE = 1
AT_UP = 2
AT_PANEL = 3
AT_A2A = 5
AT_ROWS = AT_A2A + NZ
AT_HID = AT_ROWS + RING * GROUPS
AT_SIB = AT_HID + RING * GROUPS
AT_COUNT = AT_SIB + GROUPS
AT_TOTAL = AT_COUNT + NZ
AT_CAST = AT_TOTAL + 1
N_RECV = AT_CAST
N_SEND = AT_CAST + 2 * len(FROM_ROOT)
N_LOCAL = 11 + CHIPS


def exact(a, b):
    return jnp.dot(a, b, precision=lax.Precision.HIGHEST, preferred_element_type=jnp.float32)


def kernel(
    routes_at, tokens, gate_w, up_w, down_at, codes_at, scales_at, hinv_at,
    hess_out, err_out, down_out,
    hess, err_v, down_v, routes, down_w, codes, scales, hinv,
    tok, packed, rows, weights, hid, u_panel, w_panel, count, heard, total,
    send, recv, local,
):
    e = lax.axis_index("expert")
    f = lax.axis_index("ffn")
    xh, z = e // NZ, e % NZ
    y, xl, c = f // 4, (f // 2) % 2, f % 2
    chip = f // 2
    xo = 1 - xl
    yp, ym, yo = (y + 1) % NY, (y + 3) % NY, (y + 2) % NY
    sibling = (e, f + 1 - 2 * c)

    def chip_of(yy, xx):
        return yy * 2 + xx

    def peer(yy, xx):
        return (e, yy * 4 + xx * 2 + c)

    def far(z_to):
        return (((xh + c) % 2) * NZ + z_to, f)

    def copy(src, dst, at, device, send_at=None):
        return pltpu.make_async_remote_copy(
            src_ref=src,
            dst_ref=dst,
            send_sem=send.at[at if send_at is None else send_at],
            recv_sem=recv.at[at],
            device_id=device,
            device_id_type=MESH,
        )

    sent = []

    def go(src, dst, at, device):
        copy(src, dst, at, device).start()
        sent.append((src, at))

    def arrived(region, at):
        copy(region, region, at, sibling).wait_recv()

    half = pl.ds(pl.multiple_of(c * FEAT, FEAT), FEAT)
    other_half = pl.ds(pl.multiple_of((1 - c) * FEAT, FEAT), FEAT)
    own_tok = pltpu.make_async_copy(tokens, tok.at[half], local.at[0])
    own_gate = pltpu.make_async_copy(gate_w, weights.at[c, 0], local.at[1])
    own_up = pltpu.make_async_copy(up_w, weights.at[c, 1], local.at[2])
    small = [
        pltpu.make_async_copy(src, dst, local.at[4 + i])
        for i, (src, dst) in enumerate(
            [(routes_at, routes), (hinv_at, hinv), (down_at, down_w), (codes_at, codes), (scales_at, scales)]
        )
    ]
    small[0].start()
    own_tok.start()
    for one in small[1:]:
        one.start()
    own_gate.start()
    own_up.start()

    barrier = pltpu.get_barrier_semaphore()

    def greet(device):
        pl.semaphore_signal(barrier, inc=1, device_id=device, device_id_type=MESH)

    for dz in range(1, NZ):
        greet(far((z + dz) % NZ))

    @pl.when(c == 1)
    def _():
        greet(far(z))

    for yy in (y, yp, ym, yo):
        greet(peer(yy, xo))
    for yy in (yp, ym, yo):
        greet(peer(yy, xl))
    greet(sibling)

    small[0].wait()
    names = routes[...]
    experts = lax.broadcasted_iota(jnp.int32, (32, 128), 0)
    named = ((names[0:1, :] == experts) | (names[1:2, :] == experts)).astype(jnp.float32)
    earlier = (
        lax.broadcasted_iota(jnp.int32, (128, 128), 0) < lax.broadcasted_iota(jnp.int32, (128, 128), 1)
    ).astype(jnp.bfloat16)
    named_b = named.astype(jnp.bfloat16)
    rank = jnp.dot(named_b, earlier, preferred_element_type=jnp.float32)
    base = ((xh + c) % 2) * NZ
    slot = lax.broadcasted_iota(jnp.int32, (NZ * CAP, 32), 0)
    widen = (lax.broadcasted_iota(jnp.int32, (NZ * CAP, 32), 1) == base + slot // CAP).astype(jnp.bfloat16)
    rank_at = jnp.dot(widen, rank.astype(jnp.bfloat16), preferred_element_type=jnp.float32)
    named_at = jnp.dot(widen, named_b, preferred_element_type=jnp.float32)
    place = (lax.broadcasted_iota(jnp.int32, (NZ * CAP, 128), 0) % CAP).astype(jnp.float32)
    pick = jnp.where(rank_at == place, named_at, 0.0).astype(jnp.bfloat16)
    mine_of = (
        lax.broadcasted_iota(jnp.int32, (NZ, 32), 1) == base + lax.broadcasted_iota(jnp.int32, (NZ, 32), 0)
    ).astype(jnp.bfloat16)
    named_mine = jnp.dot(mine_of, named_b, preferred_element_type=jnp.float32)
    count[...] = jnp.dot(
        named_mine.astype(jnp.bfloat16), jnp.ones((128, 128), jnp.bfloat16), preferred_element_type=jnp.float32
    ).reshape(NZ, 1, 128)

    small[1].wait()
    small[2].wait()
    peers = NZ - 1 + CHIPS - 1 + 1

    @pl.when(c == 0)
    def _():
        pl.semaphore_wait(barrier, peers)

    @pl.when(c == 1)
    def _():
        pl.semaphore_wait(barrier, peers + 1)

    go(tokens, tok.at[half], AT_TOK, sibling)

    def cast(other):
        to = (e, jnp.int32(other))
        at = AT_CAST + 2 * FROM_ROOT.index(other)
        return copy(hinv, u_panel, AT_PANEL, to, at), copy(down_w, w_panel, AT_PANEL + 1, to, at + 1)

    @pl.when(f == 0)
    def _():
        for other in FROM_ROOT:
            for one in cast(other):
                one.start()
        u_panel[...] = hinv[...]
        w_panel[...] = down_w[...]

    own_tok.wait()
    arrived(tok.at[other_half], AT_TOK)
    packed[...] = (
        lax.dot_general(pick, tok[...], (((1,), (1,)), ((), ())), preferred_element_type=jnp.float32)
        .astype(jnp.bfloat16)
        .reshape(NZ, CAP, WIDE)
    )
    def landing(block):
        return rows.at[chip, pl.ds(block * CAP, CAP), :]

    def targets():
        for g in range(GROUPS):
            for j, dz in enumerate(Z_ORDER[g]):
                yield FIRST[g] + j, (z + dz) % NZ

    stay = pltpu.make_async_copy(packed.at[z], landing(0), local.at[3])
    cross_over = copy(packed.at[z], landing(0), AT_A2A, far(z))

    @pl.when(c == 0)
    def _():
        stay.start()

    @pl.when(c == 1)
    def _():
        cross_over.start()

    for block, z_to in targets():
        if block:
            go(packed.at[z_to], landing(block), AT_A2A + block, far(z_to))

    go(gate_w, weights.at[c, 0], AT_GATE, sibling)
    go(up_w, weights.at[c, 1], AT_UP, sibling)

    def dispatch_arrived(g):
        for block in range(FIRST[g], FIRST[g] + len(Z_ORDER[g])):
            if block == 0:

                @pl.when(c == 0)
                def _():
                    stay.wait()

                @pl.when(c == 1)
                def _():
                    arrived(landing(0), AT_A2A)
            else:
                arrived(landing(block), AT_A2A + block)

    def panel_to_sibling():
        @pl.when((c == 0) & (f != 0))
        def _():
            arrived(u_panel, AT_PANEL)
            arrived(w_panel, AT_PANEL + 1)

        @pl.when(c == 0)
        def _():
            copy(u_panel, u_panel, AT_PANEL, sibling).start()
            copy(w_panel, w_panel, AT_PANEL + 1, sibling).start()

    def counts_out():
        heard[0] = count[z]
        for block, z_to in targets():
            if block:
                go(count.at[z_to], heard.at[block], AT_COUNT + block, far(z_to))

        @pl.when(c == 1)
        def _():
            copy(count.at[z], heard.at[NZ], AT_COUNT, far(z)).start()

    def ring(piece, at, count_rows, width, cut):
        half_rows = count_rows // 2

        def part(yy, xx, first=0, count=count_rows, low=True, high=True):
            ref = piece(chip_of(yy, xx))
            start = 0 if low else cut
            stop = width if high else cut
            return ref.at[pl.ds(first, count), pl.ds(start, stop - start)]

        def send_own():
            mine = part(y, xl)
            go(mine, mine, at + 1, peer(yp, xl))
            go(mine, mine, at + 2, peer(ym, xl))
            go(mine, mine, at + 0, peer(y, xo))

        def second():
            arrived(part(y, xo), at + 0)
            low = part(y, xo, high=False)
            go(low, low, at + 5, peer(yp, xl))
            go(low, low, at + 6, peer(ym, xl))
            arrived(part(ym, xl), at + 1)
            on = part(ym, xl, 0, half_rows)
            go(on, on, at + 3, peer(yp, xl))
            cross = part(ym, xl, low=False)
            go(cross, cross, at + 9, peer(y, xo))
            arrived(part(yp, xl), at + 2)
            on = part(yp, xl, half_rows, half_rows)
            go(on, on, at + 4, peer(ym, xl))
            cross = part(yp, xl, low=False)
            go(cross, cross, at + 10, peer(y, xo))

        def third():
            arrived(part(ym, xo, high=False), at + 5)
            on = part(ym, xo, 0, half_rows, high=False)
            go(on, on, at + 7, peer(yp, xl))
            arrived(part(yp, xo, high=False), at + 6)
            on = part(yp, xo, half_rows, half_rows, high=False)
            go(on, on, at + 8, peer(ym, xl))
            arrived(part(yo, xl, 0, half_rows), at + 3)
            arrived(part(yo, xl, half_rows, half_rows), at + 4)
            cross = part(yo, xl, low=False)
            go(cross, cross, at + 11, peer(y, xo))

        def last():
            arrived(part(ym, xo, low=False), at + 9)
            arrived(part(yp, xo, low=False), at + 10)
            arrived(part(yo, xo, 0, half_rows, high=False), at + 7)
            arrived(part(yo, xo, half_rows, half_rows, high=False), at + 8)
            arrived(part(yo, xo, low=False), at + 11)

        return send_own, second, third, last

    def straight(piece, at):
        chips = [(dy, dx) for dy in (2, 1, 3, 0) for dx in (1, 0) if (dy, dx) != (0, 0)]

        def send_own():
            mine = piece(chip)
            for dy, dx in chips:
                go(mine, mine, at + dy * 2 + dx - 1, peer((y + dy) % NY, (xl + dx) % 2))

        def last():
            for dy, dx in chips:
                arrived(piece(chip_of((y + NY - dy) % NY, (xl + dx) % 2)), at + dy * 2 + dx - 1)

        def nothing():
            pass

        return send_own, nothing, nothing, last

    def weighed(g, chips):
        sums = jnp.zeros((ROWS[g], 2 * HID), jnp.float32)
        for s in chips:
            span = pl.ds(pl.multiple_of(s * WIDE, WIDE), WIDE)
            factor = jnp.concatenate(
                [weights[0, 0, span, :], weights[1, 0, span, :], weights[0, 1, span, :], weights[1, 1, span, :]],
                axis=1,
            )
            piece = rows[s, pl.ds(FIRST[g] * CAP, ROWS[g]), :]
            sums += jnp.dot(piece, factor, preferred_element_type=jnp.float32)
        return sums

    def hidden_units(g, last):
        if g == 0:
            own_gate.wait()
            own_up.wait()
            arrived(weights.at[1 - c, 0], AT_GATE)
            arrived(weights.at[1 - c, 1], AT_UP)
        early = weighed(g, [chip, chip_of(y, xo), chip_of(ym, xl), chip_of(yp, xl), chip_of(yo, xl)])
        last()
        sums = early + weighed(g, [chip_of(ym, xo), chip_of(yp, xo), chip_of(yo, xo)])
        gate, up = sums[:, :HID], sums[:, HID:]
        hid[c, chip, pl.ds(FIRST[g] * CAP, ROWS[g]), :] = (gate / (1.0 + jnp.exp(-gate)) * up).astype(jnp.bfloat16)

    def group(g):
        span_g = pl.ds(FIRST[g] * CAP, ROWS[g])

        def row_piece(s):
            return rows.at[s, span_g, :]

        def hid_piece(s):
            return hid.at[c, s, span_g, :]

        if ROWS_RING[g]:
            send_own, second, third, last = ring(row_piece, AT_ROWS + RING * g, ROWS[g], WIDE, CUT)
        else:
            send_own, second, third, last = straight(row_piece, AT_ROWS + RING * g)
        if HID_RING[g]:
            h_own, h_second, h_third, h_last = ring(hid_piece, AT_HID + RING * g, ROWS[g], HID, HCUT)
        else:
            h_own, h_second, h_third, h_last = straight(hid_piece, AT_HID + RING * g)

        def start():
            dispatch_arrived(g)
            send_own()

        def compute():
            hidden_units(g, last)
            h_own()

        def pass_on():
            h_last()
            mine = hid.at[c, :, span_g, :]
            go(mine, mine, AT_SIB + g, sibling)

        def finish():
            arrived(hid.at[1 - c, :, span_g, :], AT_SIB + g)

        return start, second, third, compute, h_second, h_third, pass_on, finish

    def panel():
        @pl.when(c == 1)
        def _():
            arrived(u_panel, AT_PANEL)
            arrived(w_panel, AT_PANEL + 1)

        u = u_panel[...]
        r = lax.broadcasted_iota(jnp.int32, (128, 128), 0)
        q = lax.broadcasted_iota(jnp.int32, (128, 128), 1)
        on_diag = r == q
        inverse = jnp.where(on_diag, 1.0 / jnp.where(on_diag, u, 1.0), 0.0)
        size = 1
        while size < 128:
            block = jnp.where((r // (2 * size) == q // (2 * size)) & (r // size != q // size), u, 0.0)
            inverse = inverse - exact(exact(inverse, block), inverse)
            size *= 2
            yield
        small[3].wait()
        small[4].wait()
        steps = jnp.sum(jnp.where(on_diag, scales[...], 0.0), axis=1, keepdims=True)
        quant = steps * (codes[...] - 8).astype(jnp.float32)
        err = exact(w_panel[...].astype(jnp.float32) - quant, inverse)
        err_v[...] = err
        yield
        rest = down_w[...].astype(jnp.float32) - exact(err, hinv[...])
        down_v[...] = jnp.where(f == 0, quant, rest).astype(jnp.bfloat16)
        for one in results[:2]:
            one.start()

    columns = [pl.ds(s * HID, HID) for s in range(CHIPS)]
    results = [
        pltpu.make_async_copy(err_v, err_out, local.at[9]),
        pltpu.make_async_copy(down_v, down_out, local.at[10]),
    ] + [
        pltpu.make_async_copy(hess.at[:, columns[s]], hess_out.at[:, columns[s]], local.at[11 + s])
        for s in range(CHIPS)
    ]

    stages = [group(g) for g in range(GROUPS)]
    solve = panel()

    def run(*order):
        for who, what in order:
            if who == SOLVE:
                for _ in range(what):
                    next(solve, None)
            else:
                stages[who][what]()

    def products(start, count):
        def take(cc, at, width_at):
            return hid[cc, at, pl.ds(start, count), width_at]

        own = pl.ds(pl.multiple_of(c * COLS, COLS), COLS)
        mine = jnp.concatenate([take(0, chip, own), take(1, chip, own)], axis=0)
        for s in range(CHIPS):
            both = jnp.concatenate([take(0, s, slice(None)), take(1, s, slice(None))], axis=0)
            yield s, lax.dot_general(mine, both, (((0,), (0,)), ((), ())), preferred_element_type=jnp.float32)

    counts_out()
    run((0, 0))
    panel_to_sibling()
    run(
        (SOLVE, 4), (0, 1), (1, 0), (SOLVE, 2), (0, 2), (1, 1), (2, 0), (SOLVE, 2), (0, 3),
        (1, 2), (2, 1), (3, 0), (SOLVE, 1), (0, 4), (1, 3), (2, 2), (3, 1), (0, 5),
        (1, 4), (2, 3), (3, 2), (0, 6), (1, 5), (2, 4), (3, 3), (1, 6), (2, 5),
        (0, 7), (2, 6), (1, 7), (2, 7),
    )

    for block in range(1, NZ):
        arrived(heard.at[block], AT_COUNT + block)

    @pl.when(c == 1)
    def _():
        arrived(heard.at[NZ], AT_COUNT)

    own_count = jnp.sum(heard[1:NZ, 0], axis=0, keepdims=True) + jnp.where(c == 0, heard[0], heard[NZ])
    total[c] = jnp.broadcast_to(own_count, (8, 128))
    go(total.at[c], total.at[c], AT_TOTAL, sibling)
    for s, product in products(0, LATE):
        hess[:, columns[s]] = product
    run((3, 6))
    arrived(total.at[1 - c], AT_TOTAL)
    scale = 2.0 / (total[0, 0:1, :] + total[1, 0:1, :])
    scale = jnp.concatenate([scale, scale], axis=1)
    run((3, 7))
    for s, product in products(LATE, ROWS[-1]):
        hess[:, columns[s]] = scale * (hess[:, columns[s]] + product)
        results[2 + s].start()

    for src, at in sent:
        copy(src, src, at, sibling).wait_send()

    @pl.when(c == 1)
    def _():
        cross_over.wait_send()
        copy(count.at[z], heard.at[NZ], AT_COUNT, far(z)).wait_send()

    @pl.when(c == 0)
    def _():
        copy(u_panel, u_panel, AT_PANEL, sibling).wait_send()
        copy(w_panel, w_panel, AT_PANEL + 1, sibling).wait_send()

    @pl.when(f == 0)
    def _():
        for other in FROM_ROOT:
            for one in cast(other):
                one.wait_send()

    for one in results:
        one.wait()


def hand_on(hess, err, down, hess_out, err_out, down_out, hess_v, err_v, down_v, in_sems, out_sems):
    part = 32
    trips = [(err, err_v, err_out), (down, down_v, down_out)]
    for i in range(4):
        span = pl.ds(i * part, part)
        trips.append((hess.at[span], hess_v.at[span], hess_out.at[span]))
    loads = [pltpu.make_async_copy(src, here, in_sems.at[i]) for i, (src, here, _) in enumerate(trips)]
    stores = [pltpu.make_async_copy(here, dst, out_sems.at[i]) for i, (_, here, dst) in enumerate(trips)]
    for load in loads:
        load.start()
    for load, store in zip(loads, stores):
        load.wait()
        store.start()
    for store in stores:
        store.wait()


def body(tokens, routes, gate_w, up_w, down_w, codes, scales, hinv_panel):
    hbm = pl.BlockSpec(memory_space=pltpu.HBM)
    outs = (
        jax.ShapeDtypeStruct((COLS, 2048), jnp.float32),
        jax.ShapeDtypeStruct((128, 128), jnp.float32),
        jax.ShapeDtypeStruct((128, 128), jnp.bfloat16),
    )
    done = pl.pallas_call(
        kernel,
        out_shape=outs,
        in_specs=[hbm] * 8,
        out_specs=(hbm,) * 3,
        scratch_shapes=[
            pltpu.VMEM((COLS, 2048), jnp.float32),
            pltpu.VMEM((128, 128), jnp.float32),
            pltpu.VMEM((128, 128), jnp.bfloat16),
            pltpu.VMEM((2, 128), jnp.int32),
            pltpu.VMEM((128, 128), jnp.bfloat16),
            pltpu.VMEM((128, 128), jnp.int32),
            pltpu.VMEM((1, 128), jnp.float32),
            pltpu.VMEM((128, 128), jnp.float32),
            pltpu.VMEM((WIDE, 128), jnp.bfloat16),
            pltpu.VMEM((NZ, CAP, WIDE), jnp.bfloat16),
            pltpu.VMEM((CHIPS, NZ * CAP, WIDE), jnp.bfloat16),
            pltpu.VMEM((2, 2, CHIPS * WIDE, COLS), jnp.bfloat16),
            pltpu.VMEM((2, CHIPS, NZ * CAP, HID), jnp.bfloat16),
            pltpu.VMEM((128, 128), jnp.float32),
            pltpu.VMEM((128, 128), jnp.bfloat16),
            pltpu.VMEM((NZ, 1, 128), jnp.float32),
            pltpu.VMEM((NZ + 1, 1, 128), jnp.float32),
            pltpu.VMEM((2, 8, 128), jnp.float32),
            pltpu.SemaphoreType.DMA((N_SEND,)),
            pltpu.SemaphoreType.DMA((N_RECV,)),
            pltpu.SemaphoreType.DMA((N_LOCAL,)),
        ],
        compiler_params=pltpu.CompilerParams(
            collective_id=0, has_side_effects=True, vmem_limit_bytes=62 * 1024 * 1024
        ),
        cost_estimate=pl.CostEstimate(flops=2_200_000_000, bytes_accessed=16_000_000, transcendentals=65536),
        name="calibrate",
    )(routes.T, tokens.T, gate_w[0], up_w[0], down_w[0], codes[0], scales, hinv_panel[0])
    hess, err, down = pl.pallas_call(
        hand_on,
        out_shape=outs,
        in_specs=[hbm] * 3,
        out_specs=(hbm,) * 3,
        scratch_shapes=[
            pltpu.VMEM((COLS, 2048), jnp.float32),
            pltpu.VMEM((128, 128), jnp.float32),
            pltpu.VMEM((128, 128), jnp.bfloat16),
            pltpu.SemaphoreType.DMA((6,)),
            pltpu.SemaphoreType.DMA((6,)),
        ],
        name="hand_on",
    )(*done)
    return hess[None], err[None], down[None]


def solution(mesh):
    return jax.shard_map(
        body,
        mesh=mesh,
        in_specs=(
            P("expert", "ffn"),
            P("expert", None),
            P("expert", None, "ffn"),
            P("expert", None, "ffn"),
            P("expert", None, "ffn"),
            P("expert", None, None),
            P("expert", None),
            P("expert", None, "ffn"),
        ),
        out_specs=(P("expert", "ffn", None), P("expert", None, None), P("expert", None, "ffn")),
        check_vma=False,
    )
```
